512 devices in a mesh: expert: 64 (over y, z), tensor: 8 (over x, core).
Axes of the slice: x: 4, y: 8, z: 8, core: 2. Of those that a mesh axis runs over, the one named last changes fastest.
Arguments:
- patches: bfloat16 [32768, 1664], P('expert', 'tensor'), may hold values from -6 to 6
- expert_ids: int32 [32768, 2], P('expert'), may hold values from 0 to 63, all different within a row
- gate_values: float32 [32768, 2], P('expert'), may hold values from 0.2 to 1
- w_up: bfloat16 [64, 1664, 4096], P('expert', None, 'tensor'), may hold values from -0.15625 to 0.15625
- w_down: bfloat16 [64, 4096, 1664], P('expert', 'tensor'), may hold values from -0.09375 to 0.09375
Outputs:
- mixed: bfloat16 [32768, 1664], P('expert', 'tensor')
The draws below stay inside these ranges and needn't reach their ends.
Inputs may be any that keep to these rules, and one draw needn't show every extreme that they name: `expert_ids`: the 2 experts of a patch differ, and every expert is chosen by some patch.
All inputs are finite; a program needn't handle non-finite values.
Results may differ from the reference program's by a relative error of at most 0.019.
Values may be sent and summed in bfloat16 or wider, within the bound.
A program may use at most 128 MiB of HBM per device.

```python
import jax
import jax.numpy as jnp
from jax import lax

D = 1664
FF = 4096
TOP = 2
TOK_DEV = 512
EXPERTS = 64
TOKENS = 32768
CAP = 16
N_EXPERT = 64
N_TENSOR = 8


def block_scale(own_key, extent, pieces, least, high):
    gain = 1.0
    for axis_at, parts in pieces:
        draws = jax.random.uniform(jax.random.fold_in(jax.random.fold_in(own_key, 6), axis_at), (parts,), jnp.float32, least / len(pieces), high / len(pieces))
        gain = gain * jnp.repeat(jnp.exp(draws), extent[axis_at] // parts).reshape((-1,) + (1,) * (len(extent) - 1 - axis_at))
    return gain


def picks_of(stream_key, rows, amount, top, lift):
    ranking = jax.random.permutation(jax.random.fold_in(stream_key, 1), amount)
    favour = ranking
    for power in range(3):
        favour = favour * favour // amount
    favour = favour * lift // amount
    chance = jax.random.randint(jax.random.fold_in(stream_key, 2), (rows, amount), 0, 4096) + favour
    holders = jax.random.permutation(jax.random.fold_in(stream_key, 3), rows)[jnp.arange(amount) % rows]
    chance = jnp.where(jnp.arange(rows)[:, None] == holders[None, :], 1 << 14, chance)
    priority = chance * amount + jnp.arange(amount)
    return lax.top_k(priority.astype(jnp.int32), top)[1].astype(jnp.int32)


def gaussian(key, shape, deviation, reach, cuts=(), kind=jnp.bfloat16):
    drawn = deviation * jax.random.normal(key, shape, jnp.float32)
    if cuts:
        drawn = drawn * block_scale(key, shape, cuts, -0.22, 0.18)
    return jnp.clip(drawn, -reach, reach).astype(kind)


def setup_inputs(seed: int = 0) -> dict:
    keys = jax.random.split(jax.random.key(seed), 6)
    patches = gaussian(keys[0], (TOKENS, D), 1.0, 6.0, ((0, 64), (1, 8)))
    expert_ids = picks_of(keys[1], TOKENS, EXPERTS, TOP, 512)
    gate_values = jnp.clip(0.2 + 0.8 * jax.random.uniform(keys[2], (TOKENS, TOP), jnp.float32) ** block_scale(keys[2], (TOKENS, TOP), ((0, 64),), -0.2, 0.2), 0.2, 1.0)
    w_up = gaussian(keys[3], (EXPERTS, D, FF), D ** -0.5, 0.15625, ((0, 64), (2, 8)))
    w_down = gaussian(keys[4], (EXPERTS, FF, D), FF ** -0.5, 0.09375, ((0, 64), (1, 8)))
    return dict(patches=patches, expert_ids=expert_ids, gate_values=gate_values, w_up=w_up, w_down=w_down)


def ranks_of(expert_ids):
    blocks = expert_ids.reshape(N_EXPERT, TOK_DEV, TOP)
    onehot = (blocks[:, :, :, None] == jnp.arange(EXPERTS, dtype=jnp.int32)).astype(jnp.int32)
    ordered = jnp.transpose(onehot, (0, 2, 1, 3)).reshape(N_EXPERT, TOP * TOK_DEV, EXPERTS)
    before = jnp.cumsum(ordered, axis=1) - ordered
    rank = jnp.sum(before * ordered, axis=2).reshape(N_EXPERT, TOP, TOK_DEV)
    return jnp.transpose(rank, (0, 2, 1)).reshape(TOKENS, TOP)


def expert_apply(inputs):
    rows, up_weight, down_weight = inputs
    hidden = jax.nn.gelu(jnp.dot(rows, up_weight, preferred_element_type=jnp.float32), approximate=False).astype(jnp.bfloat16)
    group = FF // N_TENSOR
    total = jnp.zeros((rows.shape[0], D), jnp.float32)
    for index in range(N_TENSOR):
        term = jnp.dot(hidden[:, index * group:(index + 1) * group], down_weight[index * group:(index + 1) * group, :], preferred_element_type=jnp.float32)
        term = lax.optimization_barrier(term.astype(jnp.bfloat16))
        total = total + term.astype(jnp.float32)
    return total.astype(jnp.bfloat16)


def reference(patches, expert_ids, gate_values, w_up, w_down):
    rank = ranks_of(expert_ids)
    source = (jnp.arange(TOKENS, dtype=jnp.int32) // TOK_DEV)[:, None]
    dump = EXPERTS * N_EXPERT * CAP
    target = (expert_ids * N_EXPERT + source) * CAP + rank
    target = jnp.where(rank < CAP, target, dump).astype(jnp.int32)
    copies = jnp.broadcast_to(patches[:, None, :], (TOKENS, TOP, D)).reshape(TOKENS * TOP, D)
    buffer = jnp.zeros((dump, D), jnp.bfloat16).at[target.reshape(-1)].set(copies, mode="drop")
    buffer = buffer.reshape(EXPERTS, N_EXPERT * CAP, D)
    expert_out = lax.map(expert_apply, (buffer, w_up, w_down)).reshape(dump, D)
    total = jnp.zeros((TOKENS, D), jnp.float32)
    for choice_index in range(TOP):
        values = jnp.take(expert_out, target[:, choice_index], axis=0, mode="fill", fill_value=0)
        total = total + gate_values[:, choice_index][:, None] * values.astype(jnp.float32)
    return total.astype(jnp.bfloat16)
```

```python
import functools

import jax
import jax.numpy as jnp
from jax import lax
from jax.experimental import pallas as pl
from jax.experimental.pallas import tpu as pltpu
from jax.sharding import PartitionSpec as P

TOP = 2
CHUNKS = 4
MESH = pl.DeviceIdType.MESH
BF16 = jnp.bfloat16
F32 = jnp.float32

OWN_R, OWN_L, FWD_R, FWD_L, SIB_OWN, SIB_L, SIB_R, SIB_FA, SIB_FB = range(9)
SIB_SUM, HALF_R, HALF_L, SUM_R, SUM_L = range(9, 14)
KINDS = 14


def erf(x):
    x = jnp.clip(x, -3.832506856900711, 3.832506856900711)
    s = x * x
    num = jnp.full_like(s, 0.00022905065861350646)
    for coef in (0.0034082910107109506, 0.050955695062380861, 0.18520832239976145, 1.128379143519084):
        num = num * s + coef
    den = jnp.full_like(s, -1.1791602954361697e-7)
    for coef in (0.000023547966471313185, 0.0010179625278914885, 0.014070470171167667, 0.11098505178285362, 0.49746925110067538, 1.0):
        den = den * s + coef
    return x * num / den


def gelu(x):
    return 0.5 * x * (1.0 + erf(x * 0.7071067811865476))


def layer_kernel(
    dims,
    patches_ref, ids_ref, gates_ref, up_hbm, down_hbm,
    out_ref,
    up_v, down_v, up_t, down_t, padded, onehot, send, rows_in, feats,
    other, from_sib, own, sums, half_l, half_r, full_l, full_r, back, rows_out,
    w_sem, a2a_send, a2a_recv, back_send, back_recv, send_sem, recv_sem,
):
    ny, nz, nt, cap, dsh, chunks = dims
    experts = ny * nz
    nx = nt // 2
    count = ids_ref.shape[1]
    slots = experts * cap
    per = experts // chunks
    repeat = per // ny
    lanes = per * cap
    width = send.shape[1]
    cut = (dsh // 16 + 1) // 2 * 16

    e = lax.axis_index("expert")
    t = lax.axis_index("tensor")
    y, z = e // nz, e % nz
    x, core = t // 2, t % 2
    right = (t + 2) % nt
    left = (t + nt - 2) % nt
    sib = x * 2 + 1 - core

    def shard_of(step, parity):
        return ((x + step) % nx) * 2 + parity

    def shift(k):
        chunk, i = k // per, k % per
        dy = i // repeat
        dz = (chunk + chunks * (i % repeat) + ny * nz - dy) % nz
        return dy, dz

    def block(at):
        return pl.ds(pl.multiple_of(at * cap, cap), cap)

    up_copy = pltpu.make_async_copy(up_hbm, up_v, w_sem.at[0])
    down_copy = pltpu.make_async_copy(down_hbm, down_v, w_sem.at[1])
    up_copy.start()
    down_copy.start()

    barrier = pltpu.get_barrier_semaphore()

    def greet(k, carry):
        pl.semaphore_signal(barrier, inc=1, device_id={"expert": (e + k) % experts}, device_id_type=MESH)
        return carry

    lax.fori_loop(1, experts, greet, 0)
    for partner in (right, left, sib):
        pl.semaphore_signal(barrier, inc=1, device_id={"tensor": partner}, device_id_type=MESH)

    padded[...] = jnp.zeros_like(padded)
    padded[0:dsh, :] = patches_ref[...]
    earlier = (
        lax.broadcasted_iota(jnp.int32, (count, count), 0) < lax.broadcasted_iota(jnp.int32, (count, count), 1)
    ).astype(F32).astype(BF16)
    expert_row = lax.broadcasted_iota(jnp.int32, (experts, count), 0)
    targets = []
    taken = jnp.zeros((experts, 1), F32)
    for k in range(TOP):
        ids = ids_ref[k:k + 1, :]
        hot = (expert_row == ids).astype(F32)
        before = jnp.dot(hot.astype(BF16), earlier, preferred_element_type=F32) + taken
        rank = jnp.sum(hot * before, axis=0, keepdims=True)
        taken = taken + jnp.sum(hot, axis=1, keepdims=True)
        targets.append(jnp.where(rank < cap, ids.astype(F32) * cap + rank, -1.0))

    tile = min(256, slots)

    def place(i, carry):
        at = pl.ds(pl.multiple_of(i * tile, tile), tile)
        slot = (lax.broadcasted_iota(jnp.int32, (tile, count), 0) + i * tile).astype(F32)
        both = jnp.zeros((tile, count), F32)
        for k in range(TOP):
            hit = (slot == targets[k]).astype(F32)
            onehot[k, at, :] = hit.astype(BF16)
            both = both + hit
        send[at, :] = lax.dot_general(
            both.astype(BF16), padded[...], (((1,), (1,)), ((), ())), preferred_element_type=F32
        ).astype(BF16)
        return carry

    lax.fori_loop(0, slots // tile, place, 0)

    pl.semaphore_wait(barrier, experts - 1 + 3)

    def out_copy(k):
        dy, dz = shift(k)
        to = ((y + dy) % ny) * nz + (z + dz) % nz
        return pltpu.make_async_remote_copy(
            src_ref=send.at[block(to)], dst_ref=rows_in.at[block(k)],
            send_sem=a2a_send, recv_sem=a2a_recv.at[k // per],
            device_id={"expert": to}, device_id_type=MESH,
        )

    def back_copy(k):
        dy, dz = shift(k)
        to = ((y + ny - dy) % ny) * nz + (z + nz - dz) % nz
        return pltpu.make_async_remote_copy(
            src_ref=back.at[block(k)], dst_ref=rows_out.at[block(e)],
            send_sem=back_send, recv_sem=back_recv,
            device_id={"expert": to}, device_id_type=MESH,
        )

    def send_out(k, carry):
        out_copy(k).start()
        return carry

    lax.fori_loop(1, experts, send_out, 0)
    rows_in[0:cap, :] = send[block(e), :]

    up_copy.wait()
    up_t[...] = up_v[...].T
    down_copy.wait()
    down_t[...] = down_v[...].T

    def shard(step, parity, first=0, size=None):
        size = dsh if size is None else size
        return pl.ds(pl.multiple_of(shard_of(step, parity) * dsh + first, 16), size)

    def push(kind, c, src, dst, partner):
        return pltpu.make_async_remote_copy(
            src_ref=src, dst_ref=dst, send_sem=send_sem.at[kind, c], recv_sem=recv_sem.at[kind, c],
            device_id={"tensor": partner}, device_id_type=MESH,
        )

    def gather_copy(kind, c):
        step, first, size, partner = {
            OWN_R: (0, 0, dsh, right),
            OWN_L: (0, 0, dsh, left),
            FWD_R: (nx - 1, 0, cut, right),
            FWD_L: (1, cut, dsh - cut, left),
            SIB_OWN: (0, 0, dsh, sib),
            SIB_L: (nx - 1, 0, dsh, sib),
            SIB_R: (1, 0, dsh, sib),
            SIB_FA: (2, 0, cut, sib),
            SIB_FB: (2, cut, dsh - cut, sib),
        }[kind]
        ref = feats.at[c, shard(step, core, first, size)]
        return push(kind, c, ref, ref, partner)

    def sum_copy(kind, c):
        if kind == SIB_SUM:
            return push(kind, c, other.at[c], from_sib.at[c], sib)
        if kind == HALF_R:
            return push(kind, c, sums.at[c, 2, pl.ds(0, cut)], half_l.at[c], right)
        if kind == HALF_L:
            return push(kind, c, sums.at[c, 2, pl.ds(cut, dsh - cut)], half_r.at[c], left)
        if kind == SUM_R:
            return push(kind, c, sums.at[c, 1], full_l.at[c], right)
        return push(kind, c, sums.at[c, nx - 1], full_r.at[c], left)

    def chunk_rows(c):
        return pl.ds(pl.multiple_of(c * lanes, lanes), lanes)

    def arrive(c):
        @pl.when(c == 0)
        def _():
            ref = rows_in.at[pl.ds(cap, lanes - cap)]
            pltpu.make_async_copy(ref, ref, a2a_recv.at[0]).wait()

        @pl.when(c > 0)
        def _():
            ref = rows_in.at[chunk_rows(c)]
            pltpu.make_async_copy(ref, ref, a2a_recv.at[c]).wait()

        turned = rows_in[chunk_rows(c), :].T
        feats[c, shard(0, core), :] = turned[0:dsh, :]
        for kind in (OWN_R, OWN_L, SIB_OWN):
            gather_copy(kind, c).start()

    def forward(c):
        gather_copy(OWN_R, c).wait_recv()
        gather_copy(FWD_R, c).start()
        gather_copy(SIB_L, c).start()
        gather_copy(OWN_L, c).wait_recv()
        gather_copy(FWD_L, c).start()
        gather_copy(SIB_R, c).start()

    def forward_last(c):
        gather_copy(FWD_R, c).wait_recv()
        gather_copy(SIB_FA, c).start()
        gather_copy(FWD_L, c).wait_recv()
        gather_copy(SIB_FB, c).start()

    def compute(c):
        for kind in (SIB_OWN, SIB_L, SIB_R, SIB_FA, SIB_FB):
            gather_copy(kind, c).wait_recv()
        hidden = gelu(jnp.dot(up_t[...], feats[c], preferred_element_type=F32)).astype(BF16)
        for step in range(nx):
            other[c, step] = jnp.dot(
                down_t[shard(step, 1 - core), :], hidden, preferred_element_type=F32
            ).astype(BF16)
        sum_copy(SIB_SUM, c).start()
        for step in range(nx):
            own[c, step] = jnp.dot(down_t[shard(step, core), :], hidden, preferred_element_type=F32)

    def add_sibling(c):
        sum_copy(SIB_SUM, c).wait_recv()
        sums[c, 2] = (own[c, 2] + from_sib[c, 2].astype(F32)).astype(BF16)
        sum_copy(HALF_R, c).start()
        sum_copy(HALF_L, c).start()
        for step in (0, 1, nx - 1):
            own[c, step] = own[c, step] + from_sib[c, step].astype(F32)

    def add_half(c):
        sum_copy(HALF_R, c).wait_recv()
        sums[c, 1, 0:cut] = (own[c, 1, 0:cut] + half_l[c].astype(F32)).astype(BF16)
        sums[c, 1, cut:dsh] = own[c, 1, cut:dsh].astype(BF16)
        sum_copy(SUM_R, c).start()
        sum_copy(HALF_L, c).wait_recv()
        sums[c, nx - 1, 0:cut] = own[c, nx - 1, 0:cut].astype(BF16)
        sums[c, nx - 1, cut:dsh] = (own[c, nx - 1, cut:dsh] + half_r[c].astype(F32)).astype(BF16)
        sum_copy(SUM_L, c).start()

    def finish(c):
        sum_copy(SUM_R, c).wait_recv()
        sum_copy(SUM_L, c).wait_recv()
        done = own[c, 0] + full_l[c].astype(F32) + full_r[c].astype(F32)
        if width > dsh:
            done = jnp.concatenate([done, jnp.zeros((width - dsh, lanes), F32)], axis=0)
        back[chunk_rows(c), :] = done.astype(BF16).T

        def give_back(i, carry):
            k = c * per + i

            @pl.when(k > 0)
            def _():
                back_copy(k).start()

            return carry

        lax.fori_loop(0, per, give_back, 0)

    stages = (arrive, forward, forward_last, compute, add_sibling, add_half, finish)

    def step(at, carry):
        for index, stage in enumerate(stages):
            c = at - index
            pl.when((c >= 0) & (c < chunks))(functools.partial(stage, c))
        return carry

    lax.fori_loop(0, chunks + len(stages) - 1, step, 0)

    rows_out[block(e), :] = back[0:cap, :]
    for c in range(chunks):
        for kind in range(SIB_SUM):
            gather_copy(kind, c).wait_send()
        for kind in range(SIB_SUM, KINDS):
            sum_copy(kind, c).wait_send()
    rest = pl.ds(0, slots - cap)
    pltpu.make_async_copy(send.at[rest], send.at[rest], a2a_send).wait()
    pltpu.make_async_copy(back.at[rest], back.at[rest], back_send).wait()
    pltpu.make_async_copy(rows_out.at[rest], rows_out.at[rest], back_recv).wait()

    turned = rows_out[...].T[0:dsh, :]
    total = jnp.zeros((dsh, count), F32)
    for k in range(TOP):
        total = total + gates_ref[k:k + 1, :] * jnp.dot(turned, onehot[k], preferred_element_type=F32)
    out_ref[...] = total.astype(BF16)


def local(patches, expert_ids, gate_values, w_up, w_down):
    experts = lax.axis_size("expert")
    nt = lax.axis_size("tensor")
    count, dsh = patches.shape
    width = (dsh + 127) // 128 * 128
    model, hid = w_up.shape[1:]
    cap = 21 * TOP * count // (20 * experts)
    slots = experts * cap
    ny = next(n for n in range(1, experts + 1) if n * n >= experts)
    nz = experts // ny
    chunks = min(CHUNKS, nz)
    lanes = slots // chunks
    nx = nt // 2
    cut = (dsh // 16 + 1) // 2 * 16
    vmem = pl.BlockSpec(memory_space=pltpu.VMEM)
    hbm = pl.BlockSpec(memory_space=pl.ANY)
    dma = pltpu.SemaphoreType.DMA
    mixed = pl.pallas_call(
        functools.partial(layer_kernel, (ny, nz, nt, cap, dsh, chunks)),
        out_shape=jax.ShapeDtypeStruct((dsh, count), BF16),
        in_specs=[vmem, vmem, vmem, hbm, hbm],
        out_specs=vmem,
        scratch_shapes=[
            pltpu.VMEM((model, hid), BF16),
            pltpu.VMEM((hid, model), BF16),
            pltpu.VMEM((hid, model), BF16),
            pltpu.VMEM((model, hid), BF16),
            pltpu.VMEM((width, count), BF16),
            pltpu.VMEM((TOP, slots, count), BF16),
            pltpu.VMEM((slots, width), BF16),
            pltpu.VMEM((slots, width), BF16),
            pltpu.VMEM((chunks, model, lanes), BF16),
            pltpu.VMEM((chunks, nx, dsh, lanes), BF16),
            pltpu.VMEM((chunks, nx, dsh, lanes), BF16),
            pltpu.VMEM((chunks, nx, dsh, lanes), F32),
            pltpu.VMEM((chunks, nx, dsh, lanes), BF16),
            pltpu.VMEM((chunks, cut, lanes), BF16),
            pltpu.VMEM((chunks, dsh - cut, lanes), BF16),
            pltpu.VMEM((chunks, dsh, lanes), BF16),
            pltpu.VMEM((chunks, dsh, lanes), BF16),
            pltpu.VMEM((slots, width), BF16),
            pltpu.VMEM((slots, width), BF16),
            dma((2,)),
            dma,
            dma((chunks,)),
            dma,
            dma,
            dma((KINDS, chunks)),
            dma((KINDS, chunks)),
        ],
        compiler_params=pltpu.CompilerParams(
            collective_id=0, has_side_effects=True, vmem_limit_bytes=50 * 1024 * 1024
        ),
        cost_estimate=pl.CostEstimate(
            flops=4 * slots * model * hid, bytes_accessed=4 * model * hid, transcendentals=0
        ),
    )(patches.T, expert_ids.T, gate_values.T, w_up[0], w_down[0])
    return mixed.T


def solution(mesh):
    in_specs = (
        P("expert", "tensor"),
        P("expert", None),
        P("expert", None),
        P("expert", None, "tensor"),
        P("expert", "tensor", None),
    )
    out_specs = P("expert", "tensor")
    return jax.shard_map(local, mesh=mesh, in_specs=in_specs, out_specs=out_specs, check_vma=False)
```

```python
import functools

import jax
import jax.numpy as jnp
from jax import lax
from jax.experimental import pallas as pl
from jax.experimental.pallas import tpu as pltpu
from jax.sharding import PartitionSpec as P

TOP = 2
VMEM_LIMIT = 60 * 1024 * 1024
MESH = pl.DeviceIdType.MESH
BF16 = jnp.bfloat16
F32 = jnp.float32

OWN_RA, OWN_RB, OWN_LA, OWN_LB, FWD_R, FWD_L, SIB_OWN, SIB_L, SIB_R, SIB_FA, SIB_FB = range(11)
SIB_HID, HALF_R, HALF_L, SUM_RA, SUM_RB, SUM_LA, SUM_LB, SIB_DOWN = range(11, 19)
KINDS = 19

GATHER = (2, 2, 2, 2)
HIDDEN = (2, 2, 2, 2)
RETURN = (2, 2, 2, 2)
ORDER = (
    ("A", 0), ("A", 1), ("F", 0), ("F", 1), ("A", 2), ("L", 0),
    ("A", 3), ("L", 1), ("U", 0), ("F", 2), ("U", 1), ("F", 3),
    ("D", 0), ("L", 2), ("D", 1), ("U", 2), ("L", 3), ("H", 0),
    ("D", 2), ("H", 1), ("U", 3), ("E", 0), ("H", 2), ("D", 3),
    ("E", 1), ("E", 2), ("H", 3), ("E", 3),
)


def gelu(x):
    return 0.5 * x * (1.0 + lax.erf(x * 0.7071067811865476))


def pieces_of(sizes):
    starts = [sum(sizes[:i]) for i in range(len(sizes))]
    return list(zip(starts, sizes))


def plan(groups):
    if groups == sum(GATHER):
        return GATHER, HIDDEN, RETURN, ORDER
    ones = (1,) * groups
    return ones, ones, ones, tuple((op, at) for at in range(groups) for op in "AFLUDHE")


def layer_kernel(
    dims, pieces, order,
    patches_hbm, ids_hbm, gates_hbm, up_hbm, down_hbm,
    out_ref,
    patches_v, ids_v, gates_v, up_v, down_v, up_t, down_t, down_all,
    onehot, send, rows_in, feats, hid, acc, sums, half_l, half_r, full_l, full_r, back, rows_out,
    in_sem, a2a_send, a2a_recv, back_send, back_recv, send_sem, recv_sem,
):
    ny, nz, nt, cap, dsh, hidden = dims
    gather_at, hidden_at, return_at = pieces
    experts = ny * nz
    nx = nt // 2
    count = ids_v.shape[1]
    slots = experts * cap
    unit = ny * cap
    width = send.shape[1]
    cut = (dsh // 16 + 1) // 2 * 16

    e = lax.axis_index("expert")
    t = lax.axis_index("tensor")
    y, z = e // nz, e % nz
    x, core = t // 2, t % 2
    right = (t + 2) % nt
    left = (t + nt - 2) % nt
    sib = x * 2 + 1 - core

    loads = [
        pltpu.make_async_copy(src, dst, in_sem.at[i])
        for i, (src, dst) in enumerate((
            (ids_hbm, ids_v), (patches_hbm, patches_v.at[pl.ds(0, dsh)]), (gates_hbm, gates_v),
            (up_hbm, up_v), (down_hbm, down_v),
        ))
    ]
    for load in loads[:2]:
        load.start()

    barrier = pltpu.get_barrier_semaphore()

    def greet(k, carry):
        pl.semaphore_signal(barrier, inc=1, device_id={"expert": (e + k) % experts}, device_id_type=MESH)
        return carry

    lax.fori_loop(1, experts, greet, 0)
    for partner in (right, left, sib):
        pl.semaphore_signal(barrier, inc=1, device_id={"tensor": partner}, device_id_type=MESH)

    for load in loads[2:]:
        load.start()

    def shard_of(step, parity):
        return ((x + step) % nx) * 2 + parity

    def shift(k):
        dy = k % ny
        dz = (k // ny + ny * nz - dy) % nz
        return dy, dz

    def block(at):
        return pl.ds(pl.multiple_of(at * cap, cap), cap)

    def lanes(piece):
        start, size = piece
        return pl.ds(start * unit, size * unit)

    if width > dsh:
        patches_v[dsh:width, :] = jnp.zeros((width - dsh, count), BF16)
    earlier = (
        lax.broadcasted_iota(jnp.int32, (count, count), 0) < lax.broadcasted_iota(jnp.int32, (count, count), 1)
    ).astype(F32).astype(BF16)
    expert_row = lax.broadcasted_iota(jnp.int32, (experts, count), 0)
    targets = []
    taken = jnp.zeros((experts, 1), F32)
    loads[0].wait()
    for k in range(TOP):
        ids = ids_v[k:k + 1, :]
        hot = (expert_row == ids).astype(F32)
        before = jnp.dot(hot.astype(BF16), earlier, preferred_element_type=F32) + taken
        rank = jnp.sum(hot * before, axis=0, keepdims=True)
        taken = taken + jnp.sum(hot, axis=1, keepdims=True)
        targets.append(jnp.where(rank < cap, ids.astype(F32) * cap + rank, -1.0))
    loads[1].wait()

    tile = min(256, slots)

    def place(i, carry):
        at = pl.ds(pl.multiple_of(i * tile, tile), tile)
        slot = (lax.broadcasted_iota(jnp.int32, (tile, count), 0) + i * tile).astype(F32)
        both = jnp.zeros((tile, count), F32)
        for k in range(TOP):
            hit = (slot == targets[k]).astype(F32)
            onehot[k, at, :] = hit.astype(BF16)
            both = both + hit
        send[at, :] = lax.dot_general(
            both.astype(BF16), patches_v[...], (((1,), (1,)), ((), ())), preferred_element_type=F32
        ).astype(BF16)
        return carry

    lax.fori_loop(0, slots // tile, place, 0)

    pl.semaphore_wait(barrier, experts - 1 + 3)

    for index, (start, size) in enumerate(gather_at):
        def send_out(k, carry, index=index):
            dy, dz = shift(k)
            to = ((y + dy) % ny) * nz + (z + dz) % nz
            pltpu.make_async_remote_copy(
                src_ref=send.at[block(to)], dst_ref=rows_in.at[block(k)],
                send_sem=a2a_send, recv_sem=a2a_recv.at[index],
                device_id={"expert": to}, device_id_type=MESH,
            ).start()
            return carry

        lax.fori_loop(max(1, start * ny), (start + size) * ny, send_out, 0)
    rows_in[0:cap, :] = send[block(e), :]

    def push(kind, c, src, dst, partner):
        return pltpu.make_async_remote_copy(
            src_ref=src, dst_ref=dst, send_sem=send_sem.at[kind, c], recv_sem=recv_sem.at[kind, c],
            device_id={"tensor": partner}, device_id_type=MESH,
        )

    def shard(step, parity, first=0, size=None):
        size = dsh if size is None else size
        return pl.ds(pl.multiple_of(shard_of(step, parity) * dsh + first, 16), size)

    theirs = pl.ds(hidden, hidden)
    down_copies = [
        push(SIB_DOWN, step, down_t.at[shard(step, 1 - core)], down_all.at[pl.ds(step * dsh, dsh), theirs], sib)
        for step in range(nx)
    ]
    loads[4].wait()
    down_t[...] = down_v[...].T
    for step in range(nx):
        down_copies[step].start()
        down_all[step * dsh:(step + 1) * dsh, 0:hidden] = down_t[shard(step, core), :]
    loads[3].wait()
    up_t[...] = up_v[...].T
    loads[2].wait()

    def gather_copy(kind, c):
        step, first, size, partner = {
            OWN_RA: (0, 0, cut, right),
            OWN_RB: (0, cut, dsh - cut, right),
            OWN_LA: (0, 0, cut, left),
            OWN_LB: (0, cut, dsh - cut, left),
            FWD_R: (nx - 1, 0, cut, right),
            FWD_L: (1, cut, dsh - cut, left),
            SIB_OWN: (0, 0, dsh, sib),
            SIB_L: (nx - 1, 0, dsh, sib),
            SIB_R: (1, 0, dsh, sib),
            SIB_FA: (2, 0, cut, sib),
            SIB_FB: (2, cut, dsh - cut, sib),
        }[kind]
        ref = feats.at[shard(step, core, first, size), lanes(gather_at[c])]
        return push(kind, c, ref, ref, partner)

    def hid_copy(c):
        at = lanes(hidden_at[c])
        return push(SIB_HID, c, hid.at[pl.ds(0, hidden), at], hid.at[theirs, at], sib)

    def sum_copy(kind, c):
        at = lanes(return_at[c])
        if kind == HALF_R:
            return push(kind, c, sums.at[2, pl.ds(0, cut), at], half_l.at[:, at], right)
        if kind == HALF_L:
            return push(kind, c, sums.at[2, pl.ds(cut, dsh - cut), at], half_r.at[:, at], left)
        place, ref, partner = (1, full_l, right) if kind in (SUM_RA, SUM_RB) else (0, full_r, left)
        rows = pl.ds(0, cut) if kind in (SUM_RA, SUM_LA) else pl.ds(cut, dsh - cut)
        return push(kind, c, sums.at[place, rows, at], ref.at[rows, at], partner)

    def arrive(c):
        start, size = gather_at[c]
        own = cap if start == 0 else 0
        ref = rows_in.at[pl.ds(start * unit + own, size * unit - own)]
        pltpu.make_async_copy(ref, ref, a2a_recv.at[c]).wait()
        turned = rows_in[start * unit:(start + size) * unit, :].T
        feats[shard(0, core), lanes(gather_at[c])] = turned[0:dsh, :]
        for kind in (OWN_RA, OWN_LB, OWN_RB, OWN_LA, SIB_OWN):
            gather_copy(kind, c).start()

    def forward(c):
        gather_copy(OWN_RA, c).wait_recv()
        gather_copy(FWD_R, c).start()
        gather_copy(OWN_LB, c).wait_recv()
        gather_copy(FWD_L, c).start()

    def to_sibling(c):
        gather_copy(OWN_RB, c).wait_recv()
        gather_copy(SIB_L, c).start()
        gather_copy(OWN_LA, c).wait_recv()
        gather_copy(SIB_R, c).start()
        gather_copy(FWD_R, c).wait_recv()
        gather_copy(SIB_FA, c).start()
        gather_copy(FWD_L, c).wait_recv()
        gather_copy(SIB_FB, c).start()

    gathered = set()

    def overlaps(piece, other):
        return piece[0] < other[0] + other[1] and other[0] < piece[0] + piece[1]

    def up(c):
        for i, piece in enumerate(gather_at):
            if overlaps(piece, hidden_at[c]) and i not in gathered:
                gathered.add(i)
                for kind in (SIB_OWN, SIB_L, SIB_R, SIB_FA, SIB_FB):
                    gather_copy(kind, i).wait_recv()
        at = lanes(hidden_at[c])
        hid[0:hidden, at] = gelu(jnp.dot(up_t[...], feats[:, at], preferred_element_type=F32)).astype(BF16)
        hid_copy(c).start()

    exchanged = set()

    def down(c):
        if not exchanged:
            for copy in down_copies:
                copy.wait_recv()
        for i, piece in enumerate(hidden_at):
            if overlaps(piece, return_at[c]) and i not in exchanged:
                exchanged.add(i)
                hid_copy(i).wait_recv()
        at = lanes(return_at[c])

        def term(step):
            return jnp.dot(down_all[step * dsh:(step + 1) * dsh, :], hid[:, at], preferred_element_type=F32)

        sums[2, :, at] = term(2).astype(BF16)
        sum_copy(HALF_R, c).start()
        sum_copy(HALF_L, c).start()
        one = term(1)
        sums[1, cut:dsh, at] = one[cut:dsh].astype(BF16)
        sum_copy(SUM_RB, c).start()
        acc[1, 0:cut, at] = one[0:cut]
        last = term(nx - 1)
        sums[0, 0:cut, at] = last[0:cut].astype(BF16)
        sum_copy(SUM_LA, c).start()
        acc[1, cut:dsh, at] = last[cut:dsh]
        acc[0, :, at] = term(0)

    def add_half(c):
        at = lanes(return_at[c])
        sum_copy(HALF_R, c).wait_recv()
        sums[1, 0:cut, at] = (acc[1, 0:cut, at] + half_l[:, at].astype(F32)).astype(BF16)
        sum_copy(SUM_RA, c).start()
        sum_copy(HALF_L, c).wait_recv()
        sums[0, cut:dsh, at] = (acc[1, cut:dsh, at] + half_r[:, at].astype(F32)).astype(BF16)
        sum_copy(SUM_LB, c).start()

    def finish(c):
        start, size = return_at[c]
        at = lanes(return_at[c])
        for kind in (SUM_RA, SUM_RB, SUM_LA, SUM_LB):
            sum_copy(kind, c).wait_recv()
        done = acc[0, :, at] + full_l[:, at].astype(F32) + full_r[:, at].astype(F32)
        if width > dsh:
            done = jnp.concatenate([done, jnp.zeros((width - dsh, size * unit), F32)], axis=0)
        back[start * unit:(start + size) * unit, :] = done.astype(BF16).T

        def give_back(k, carry):
            dy, dz = shift(k)
            to = ((y + ny - dy) % ny) * nz + (z + nz - dz) % nz
            pltpu.make_async_remote_copy(
                src_ref=back.at[block(k)], dst_ref=rows_out.at[block(e)],
                send_sem=back_send, recv_sem=back_recv,
                device_id={"expert": to}, device_id_type=MESH,
            ).start()
            return carry

        lax.fori_loop(max(1, start * ny), (start + size) * ny, give_back, 0)

    stages = dict(A=arrive, F=forward, L=to_sibling, U=up, D=down, H=add_half, E=finish)
    for op, c in order:
        stages[op](c)

    rows_out[block(e), :] = back[0:cap, :]
    for copy in down_copies:
        copy.wait_send()
    for c in range(len(gather_at)):
        for kind in range(SIB_HID):
            gather_copy(kind, c).wait_send()
    for c in range(len(hidden_at)):
        hid_copy(c).wait_send()
    for c in range(len(return_at)):
        for kind in (HALF_R, HALF_L, SUM_RA, SUM_RB, SUM_LA, SUM_LB):
            sum_copy(kind, c).wait_send()
    rest = pl.ds(0, slots - cap)
    pltpu.make_async_copy(send.at[rest], send.at[rest], a2a_send).wait()
    pltpu.make_async_copy(back.at[rest], back.at[rest], back_send).wait()
    pltpu.make_async_copy(rows_out.at[rest], rows_out.at[rest], back_recv).wait()

    turned = rows_out[...].T[0:dsh, :]
    total = jnp.zeros((dsh, count), F32)
    for k in range(TOP):
        total = total + gates_v[k:k + 1, :] * jnp.dot(turned, onehot[k], preferred_element_type=F32)
    out_ref[...] = total.astype(BF16)


def local(patches, expert_ids, gate_values, w_up, w_down):
    experts = lax.axis_size("expert")
    nt = lax.axis_size("tensor")
    count, dsh = patches.shape
    width = (dsh + 127) // 128 * 128
    model, hidden = w_up.shape[1:]
    cap = 21 * TOP * count // (20 * experts)
    slots = experts * cap
    ny = next(n for n in range(1, experts + 1) if n * n >= experts)
    nz = experts // ny
    nx = nt // 2
    cut = (dsh // 16 + 1) // 2 * 16
    gather, hiddens, returns, order = plan(nz)
    pieces = tuple(pieces_of(sizes) for sizes in (gather, hiddens, returns))
    most = max(nx, *(len(p) for p in pieces))
    hbm = pl.BlockSpec(memory_space=pl.ANY)
    dma = pltpu.SemaphoreType.DMA
    mixed = pl.pallas_call(
        functools.partial(layer_kernel, (ny, nz, nt, cap, dsh, hidden), pieces, order),
        out_shape=jax.ShapeDtypeStruct((dsh, count), BF16),
        in_specs=[hbm] * 5,
        out_specs=pl.BlockSpec(memory_space=pltpu.VMEM),
        scratch_shapes=[
            pltpu.VMEM((width, count), BF16),
            pltpu.VMEM((TOP, count), jnp.int32),
            pltpu.VMEM((TOP, count), F32),
            pltpu.VMEM((model, hidden), BF16),
            pltpu.VMEM((hidden, model), BF16),
            pltpu.VMEM((hidden, model), BF16),
            pltpu.VMEM((model, hidden), BF16),
            pltpu.VMEM((nx * dsh, 2 * hidden), BF16),
            pltpu.VMEM((TOP, slots, count), BF16),
            pltpu.VMEM((slots, width), BF16),
            pltpu.VMEM((slots, width), BF16),
            pltpu.VMEM((model, slots), BF16),
            pltpu.VMEM((2 * hidden, slots), BF16),
            pltpu.VMEM((2, dsh, slots), F32),
            pltpu.VMEM((3, dsh, slots), BF16),
            pltpu.VMEM((cut, slots), BF16),
            pltpu.VMEM((dsh - cut, slots), BF16),
            pltpu.VMEM((dsh, slots), BF16),
            pltpu.VMEM((dsh, slots), BF16),
            pltpu.VMEM((slots, width), BF16),
            pltpu.VMEM((slots, width), BF16),
            dma((5,)),
            dma,
            dma((len(gather),)),
            dma,
            dma,
            dma((KINDS, most)),
            dma((KINDS, most)),
        ],
        compiler_params=pltpu.CompilerParams(
            collective_id=0, has_side_effects=True, vmem_limit_bytes=VMEM_LIMIT
        ),
        cost_estimate=pl.CostEstimate(
            flops=4 * slots * model * hidden, bytes_accessed=4 * model * hidden, transcendentals=0
        ),
    )(patches.T, expert_ids.T, gate_values.T, w_up[0], w_down[0])
    return mixed.T


def solution(mesh):
    in_specs = (
        P("expert", "tensor"),
        P("expert", None),
        P("expert", None),
        P("expert", None, "tensor"),
        P("expert", "tensor", None),
    )
    out_specs = P("expert", "tensor")
    return jax.shard_map(local, mesh=mesh, in_specs=in_specs, out_specs=out_specs, check_vma=False)
```

```python
import functools

import jax
import jax.numpy as jnp
from jax import lax
from jax.experimental import pallas as pl
from jax.experimental.pallas import tpu as pltpu
from jax.sharding import PartitionSpec as P

TOP = 2
VMEM_LIMIT = 60 * 1024 * 1024
MESH = pl.DeviceIdType.MESH
BF16 = jnp.bfloat16
F32 = jnp.float32

OWN_RA, OWN_RB, OWN_LA, OWN_LB, FWD_R, FWD_L, SIB_OWN, SIB_L, SIB_R, SIB_FA, SIB_FB = range(11)
SIB_HID, HALF_R, HALF_L, SUM_RA, SUM_RB, SUM_LA, SUM_LB, SIB_DOWN = range(11, 19)
KINDS = 19

GATHER = (2, 2, 2, 2)
HIDDEN = (2, 2, 2, 2)
RETURN = (2, 2, 2, 2)
ORDER = (
    ("A", 0), ("A", 1), ("F", 0), ("F", 1), ("A", 2), ("L", 0),
    ("A", 3), ("L", 1), ("U", 0), ("F", 2), ("U", 1), ("F", 3),
    ("D", 0), ("L", 2), ("D", 1), ("U", 2), ("L", 3), ("H", 0),
    ("D", 2), ("H", 1), ("U", 3), ("E", 0), ("H", 2), ("D", 3),
    ("E", 1), ("E", 2), ("H", 3), ("E", 3),
)


def gelu(x):
    return 0.5 * x * (1.0 + lax.erf(x * 0.7071067811865476))


def pieces_of(sizes):
    starts = [sum(sizes[:i]) for i in range(len(sizes))]
    return list(zip(starts, sizes))


def plan(groups):
    if groups == sum(GATHER):
        return GATHER, HIDDEN, RETURN, ORDER
    ones = (1,) * groups
    return ones, ones, ones, tuple((op, at) for at in range(groups) for op in "AFLUDHE")


def farthest_first(ny, nz):
    def hops(step, size):
        return min(step, size - step)

    order = sorted((-hops(dy, ny) - hops(dz, nz), dy, dz) for dy in range(ny) for dz in range(nz))
    return [(dy, dz) for _, dy, dz in order[:-1]]


def shifts_of(ny, nz):
    far = farthest_first(ny, nz)
    parts = [far[at::4] for at in range(4)]
    parts = sorted(parts, key=len)
    return [(0, 0)] + [shift for part in parts for shift in part]


def layer_kernel(
    dims, pieces, order,
    patches_hbm, ids_hbm, gates_hbm, up_hbm, down_hbm,
    out_ref,
    patches_v, ids_v, gates_v, up_v, down_v, up_t, down_t, down_all,
    onehot, send, rows_in, feats, hid, acc, sums, half_l, half_r, full_l, full_r, back, rows_out,
    in_sem, a2a_send, a2a_recv, back_send, back_recv, send_sem, recv_sem,
):
    ny, nz, nt, cap, dsh, hidden = dims
    gather_at, hidden_at, return_at = pieces
    experts = ny * nz
    nx = nt // 2
    count = ids_v.shape[1]
    slots = experts * cap
    unit = ny * cap
    width = send.shape[1]
    cut = (dsh // 16 + 1) // 2 * 16

    e = lax.axis_index("expert")
    t = lax.axis_index("tensor")
    y, z = e // nz, e % nz
    x, core = t // 2, t % 2
    right = (t + 2) % nt
    left = (t + nt - 2) % nt
    sib = x * 2 + 1 - core

    loads = [
        pltpu.make_async_copy(src, dst, in_sem.at[i])
        for i, (src, dst) in enumerate((
            (ids_hbm, ids_v), (patches_hbm, patches_v.at[pl.ds(0, dsh)]), (gates_hbm, gates_v),
            (up_hbm, up_v), (down_hbm, down_v),
        ))
    ]
    for load in loads[:2]:
        load.start()

    barrier = pltpu.get_barrier_semaphore()

    for dy, dz in farthest_first(ny, nz):
        to = ((y + dy) % ny) * nz + (z + dz) % nz
        pl.semaphore_signal(barrier, inc=1, device_id={"expert": to}, device_id_type=MESH)
    for partner in (right, left, sib):
        pl.semaphore_signal(barrier, inc=1, device_id={"tensor": partner}, device_id_type=MESH)

    for load in loads[2:]:
        load.start()

    def shard_of(step, parity):
        return ((x + step) % nx) * 2 + parity

    shifts = shifts_of(ny, nz)

    def block(at):
        return pl.ds(at * cap if isinstance(at, int) else pl.multiple_of(at * cap, cap), cap)

    def lanes(piece):
        start, size = piece
        return pl.ds(start * unit, size * unit)

    if width > dsh:
        patches_v[dsh:width, :] = jnp.zeros((width - dsh, count), BF16)
    earlier = (
        lax.broadcasted_iota(jnp.int32, (count, count), 0) < lax.broadcasted_iota(jnp.int32, (count, count), 1)
    ).astype(F32).astype(BF16)
    expert_row = lax.broadcasted_iota(jnp.int32, (experts, count), 0)
    targets = []
    taken = jnp.zeros((experts, 1), F32)
    loads[0].wait()
    for k in range(TOP):
        ids = ids_v[k:k + 1, :]
        hot = (expert_row == ids).astype(F32)
        before = jnp.dot(hot.astype(BF16), earlier, preferred_element_type=F32) + taken
        rank = jnp.sum(hot * before, axis=0, keepdims=True)
        taken = taken + jnp.sum(hot, axis=1, keepdims=True)
        targets.append(jnp.where(rank < cap, ids.astype(F32) * cap + rank, -1.0))
    loads[1].wait()

    tile = min(256, slots)

    def place(i, carry):
        at = pl.ds(pl.multiple_of(i * tile, tile), tile)
        slot = (lax.broadcasted_iota(jnp.int32, (tile, count), 0) + i * tile).astype(F32)
        both = jnp.zeros((tile, count), F32)
        for k in range(TOP):
            hit = (slot == targets[k]).astype(F32)
            onehot[k, at, :] = hit.astype(BF16)
            both = both + hit
        send[at, :] = lax.dot_general(
            both.astype(BF16), patches_v[...], (((1,), (1,)), ((), ())), preferred_element_type=F32
        ).astype(BF16)
        return carry

    lax.fori_loop(0, slots // tile, place, 0)

    pl.semaphore_wait(barrier, experts - 1 + 3)

    for index, (start, size) in enumerate(gather_at):
        for k in range(max(1, start * ny), (start + size) * ny):
            dy, dz = shifts[k]
            to = ((y + dy) % ny) * nz + (z + dz) % nz
            pltpu.make_async_remote_copy(
                src_ref=send.at[block(to)], dst_ref=rows_in.at[block(k)],
                send_sem=a2a_send, recv_sem=a2a_recv.at[index],
                device_id={"expert": to}, device_id_type=MESH,
            ).start()
    rows_in[0:cap, :] = send[block(e), :]

    def push(kind, c, src, dst, partner):
        return pltpu.make_async_remote_copy(
            src_ref=src, dst_ref=dst, send_sem=send_sem.at[kind, c], recv_sem=recv_sem.at[kind, c],
            device_id={"tensor": partner}, device_id_type=MESH,
        )

    def shard(step, parity, first=0, size=None):
        size = dsh if size is None else size
        return pl.ds(pl.multiple_of(shard_of(step, parity) * dsh + first, 16), size)

    theirs = pl.ds(hidden, hidden)
    down_copies = [
        push(SIB_DOWN, step, down_t.at[shard(step, 1 - core)], down_all.at[pl.ds(step * dsh, dsh), theirs], sib)
        for step in range(nx)
    ]
    loads[4].wait()
    down_t[...] = down_v[...].T
    for step in range(nx):
        down_copies[step].start()
        down_all[step * dsh:(step + 1) * dsh, 0:hidden] = down_t[shard(step, core), :]
    loads[3].wait()
    up_t[...] = up_v[...].T
    loads[2].wait()

    def gather_copy(kind, c):
        step, first, size, partner = {
            OWN_RA: (0, 0, cut, right),
            OWN_RB: (0, cut, dsh - cut, right),
            OWN_LA: (0, 0, cut, left),
            OWN_LB: (0, cut, dsh - cut, left),
            FWD_R: (nx - 1, 0, cut, right),
            FWD_L: (1, cut, dsh - cut, left),
            SIB_OWN: (0, 0, dsh, sib),
            SIB_L: (nx - 1, 0, dsh, sib),
            SIB_R: (1, 0, dsh, sib),
            SIB_FA: (2, 0, cut, sib),
            SIB_FB: (2, cut, dsh - cut, sib),
        }[kind]
        ref = feats.at[shard(step, core, first, size), lanes(gather_at[c])]
        return push(kind, c, ref, ref, partner)

    def hid_copy(c):
        at = lanes(hidden_at[c])
        return push(SIB_HID, c, hid.at[pl.ds(0, hidden), at], hid.at[theirs, at], sib)

    def sum_copy(kind, c):
        at = lanes(return_at[c])
        if kind == HALF_R:
            return push(kind, c, sums.at[2, pl.ds(0, cut), at], half_l.at[:, at], right)
        if kind == HALF_L:
            return push(kind, c, sums.at[2, pl.ds(cut, dsh - cut), at], half_r.at[:, at], left)
        place, ref, partner = (1, full_l, right) if kind in (SUM_RA, SUM_RB) else (0, full_r, left)
        rows = pl.ds(0, cut) if kind in (SUM_RA, SUM_LA) else pl.ds(cut, dsh - cut)
        return push(kind, c, sums.at[place, rows, at], ref.at[rows, at], partner)

    def arrive(c):
        start, size = gather_at[c]
        own = cap if start == 0 else 0
        ref = rows_in.at[pl.ds(start * unit + own, size * unit - own)]
        pltpu.make_async_copy(ref, ref, a2a_recv.at[c]).wait()
        turned = rows_in[start * unit:(start + size) * unit, :].T
        feats[shard(0, core), lanes(gather_at[c])] = turned[0:dsh, :]
        for kind in (OWN_RA, OWN_LB, OWN_RB, OWN_LA, SIB_OWN):
            gather_copy(kind, c).start()

    def forward(c):
        gather_copy(OWN_RA, c).wait_recv()
        gather_copy(FWD_R, c).start()
        gather_copy(OWN_LB, c).wait_recv()
        gather_copy(FWD_L, c).start()

    def to_sibling(c):
        gather_copy(OWN_RB, c).wait_recv()
        gather_copy(SIB_L, c).start()
        gather_copy(OWN_LA, c).wait_recv()
        gather_copy(SIB_R, c).start()
        gather_copy(FWD_R, c).wait_recv()
        gather_copy(SIB_FA, c).start()
        gather_copy(FWD_L, c).wait_recv()
        gather_copy(SIB_FB, c).start()

    gathered = set()

    def overlaps(piece, other):
        return piece[0] < other[0] + other[1] and other[0] < piece[0] + piece[1]

    def up(c):
        for i, piece in enumerate(gather_at):
            if overlaps(piece, hidden_at[c]) and i not in gathered:
                gathered.add(i)
                for kind in (SIB_OWN, SIB_L, SIB_R, SIB_FA, SIB_FB):
                    gather_copy(kind, i).wait_recv()
        at = lanes(hidden_at[c])
        hid[0:hidden, at] = gelu(jnp.dot(up_t[...], feats[:, at], preferred_element_type=F32)).astype(BF16)
        hid_copy(c).start()

    exchanged = set()

    def down(c):
        if not exchanged:
            for copy in down_copies:
                copy.wait_recv()
        for i, piece in enumerate(hidden_at):
            if overlaps(piece, return_at[c]) and i not in exchanged:
                exchanged.add(i)
                hid_copy(i).wait_recv()
        at = lanes(return_at[c])

        def term(step):
            return jnp.dot(down_all[step * dsh:(step + 1) * dsh, :], hid[:, at], preferred_element_type=F32)

        sums[2, :, at] = term(2).astype(BF16)
        sum_copy(HALF_R, c).start()
        sum_copy(HALF_L, c).start()
        one = term(1)
        sums[1, cut:dsh, at] = one[cut:dsh].astype(BF16)
        sum_copy(SUM_RB, c).start()
        acc[1, 0:cut, at] = one[0:cut]
        last = term(nx - 1)
        sums[0, 0:cut, at] = last[0:cut].astype(BF16)
        sum_copy(SUM_LA, c).start()
        acc[1, cut:dsh, at] = last[cut:dsh]
        acc[0, :, at] = term(0)

    def add_half(c):
        at = lanes(return_at[c])
        sum_copy(HALF_R, c).wait_recv()
        sums[1, 0:cut, at] = (acc[1, 0:cut, at] + half_l[:, at].astype(F32)).astype(BF16)
        sum_copy(SUM_RA, c).start()
        sum_copy(HALF_L, c).wait_recv()
        sums[0, cut:dsh, at] = (acc[1, cut:dsh, at] + half_r[:, at].astype(F32)).astype(BF16)
        sum_copy(SUM_LB, c).start()

    def finish(c):
        start, size = return_at[c]
        at = lanes(return_at[c])
        for kind in (SUM_RA, SUM_RB, SUM_LA, SUM_LB):
            sum_copy(kind, c).wait_recv()
        done = acc[0, :, at] + full_l[:, at].astype(F32) + full_r[:, at].astype(F32)
        if width > dsh:
            done = jnp.concatenate([done, jnp.zeros((width - dsh, size * unit), F32)], axis=0)
        back[start * unit:(start + size) * unit, :] = done.astype(BF16).T

        for k in range(max(1, start * ny), (start + size) * ny):
            dy, dz = shifts[k]
            to = ((y + ny - dy) % ny) * nz + (z + nz - dz) % nz
            pltpu.make_async_remote_copy(
                src_ref=back.at[block(k)], dst_ref=rows_out.at[block(e)],
                send_sem=back_send, recv_sem=back_recv,
                device_id={"expert": to}, device_id_type=MESH,
            ).start()

    stages = dict(A=arrive, F=forward, L=to_sibling, U=up, D=down, H=add_half, E=finish)
    for op, c in order:
        stages[op](c)

    rows_out[block(e), :] = back[0:cap, :]
    for copy in down_copies:
        copy.wait_send()
    for c in range(len(gather_at)):
        for kind in range(SIB_HID):
            gather_copy(kind, c).wait_send()
    for c in range(len(hidden_at)):
        hid_copy(c).wait_send()
    for c in range(len(return_at)):
        for kind in (HALF_R, HALF_L, SUM_RA, SUM_RB, SUM_LA, SUM_LB):
            sum_copy(kind, c).wait_send()
    rest = pl.ds(0, slots - cap)
    pltpu.make_async_copy(send.at[rest], send.at[rest], a2a_send).wait()
    pltpu.make_async_copy(back.at[rest], back.at[rest], back_send).wait()
    pltpu.make_async_copy(rows_out.at[rest], rows_out.at[rest], back_recv).wait()

    turned = rows_out[...].T[0:dsh, :]
    total = jnp.zeros((dsh, count), F32)
    for k in range(TOP):
        total = total + gates_v[k:k + 1, :] * jnp.dot(turned, onehot[k], preferred_element_type=F32)
    out_ref[...] = total.astype(BF16)


def local(patches, expert_ids, gate_values, w_up, w_down):
    experts = lax.axis_size("expert")
    nt = lax.axis_size("tensor")
    count, dsh = patches.shape
    width = (dsh + 127) // 128 * 128
    model, hidden = w_up.shape[1:]
    cap = 21 * TOP * count // (20 * experts)
    slots = experts * cap
    ny = next(n for n in range(1, experts + 1) if n * n >= experts)
    nz = experts // ny
    nx = nt // 2
    cut = (dsh // 16 + 1) // 2 * 16
    gather, hiddens, returns, order = plan(nz)
    pieces = tuple(pieces_of(sizes) for sizes in (gather, hiddens, returns))
    most = max(nx, *(len(p) for p in pieces))
    hbm = pl.BlockSpec(memory_space=pl.ANY)
    dma = pltpu.SemaphoreType.DMA
    mixed = pl.pallas_call(
        functools.partial(layer_kernel, (ny, nz, nt, cap, dsh, hidden), pieces, order),
        out_shape=jax.ShapeDtypeStruct((dsh, count), BF16),
        in_specs=[hbm] * 5,
        out_specs=pl.BlockSpec(memory_space=pltpu.VMEM),
        scratch_shapes=[
            pltpu.VMEM((width, count), BF16),
            pltpu.VMEM((TOP, count), jnp.int32),
            pltpu.VMEM((TOP, count), F32),
            pltpu.VMEM((model, hidden), BF16),
            pltpu.VMEM((hidden, model), BF16),
            pltpu.VMEM((hidden, model), BF16),
            pltpu.VMEM((model, hidden), BF16),
            pltpu.VMEM((nx * dsh, 2 * hidden), BF16),
            pltpu.VMEM((TOP, slots, count), BF16),
            pltpu.VMEM((slots, width), BF16),
            pltpu.VMEM((slots, width), BF16),
            pltpu.VMEM((model, slots), BF16),
            pltpu.VMEM((2 * hidden, slots), BF16),
            pltpu.VMEM((2, dsh, slots), F32),
            pltpu.VMEM((3, dsh, slots), BF16),
            pltpu.VMEM((cut, slots), BF16),
            pltpu.VMEM((dsh - cut, slots), BF16),
            pltpu.VMEM((dsh, slots), BF16),
            pltpu.VMEM((dsh, slots), BF16),
            pltpu.VMEM((slots, width), BF16),
            pltpu.VMEM((slots, width), BF16),
            dma((5,)),
            dma,
            dma((len(gather),)),
            dma,
            dma,
            dma((KINDS, most)),
            dma((KINDS, most)),
        ],
        compiler_params=pltpu.CompilerParams(
            collective_id=0, has_side_effects=True, vmem_limit_bytes=VMEM_LIMIT
        ),
        cost_estimate=pl.CostEstimate(
            flops=4 * slots * model * hidden, bytes_accessed=4 * model * hidden, transcendentals=0
        ),
    )(patches.T, expert_ids.T, gate_values.T, w_up[0], w_down[0])
    return mixed.T


def solution(mesh):
    in_specs = (
        P("expert", "tensor"),
        P("expert", None),
        P("expert", None),
        P("expert", None, "tensor"),
        P("expert", "tensor", None),
    )
    out_specs = P("expert", "tensor")
    return jax.shard_map(local, mesh=mesh, in_specs=in_specs, out_specs=out_specs, check_vma=False)
```

```python
import functools

import jax
import jax.numpy as jnp
from jax import lax
from jax.experimental import pallas as pl
from jax.experimental.pallas import tpu as pltpu
from jax.sharding import PartitionSpec as P

TOP = 2
VMEM_LIMIT = 60 * 1024 * 1024
MESH = pl.DeviceIdType.MESH
BF16 = jnp.bfloat16
F32 = jnp.float32

OWN_RA, OWN_RB, OWN_LA, OWN_LB, FWD_R, FWD_L, SIB_OWN, SIB_L, SIB_R, SIB_FA, SIB_FB = range(11)
SIB_HID, HALF_R, HALF_L, SUM_RA, SUM_RB, SUM_LA, SUM_LB, SIB_DOWN = range(11, 19)
KINDS = 19

GATHER = (2, 2, 2, 2)
HIDDEN = (2, 2, 2, 2)
RETURN = (2, 2, 2, 2)
ORDER = (
    ("A", 0), ("A", 1), ("F", 0), ("F", 1), ("A", 2), ("L", 0),
    ("A", 3), ("L", 1), ("U", 0), ("F", 2), ("U", 1), ("F", 3),
    ("D", 0), ("L", 2), ("D", 1), ("U", 2), ("L", 3), ("H", 0),
    ("D", 2), ("H", 1), ("U", 3), ("E", 0), ("H", 2), ("D", 3),
    ("E", 1), ("E", 2), ("H", 3), ("E", 3),
)


def gelu(x):
    return 0.5 * x * (1.0 + lax.erf(x * 0.7071067811865476))


def pieces_of(sizes):
    starts = [sum(sizes[:i]) for i in range(len(sizes))]
    return list(zip(starts, sizes))


def plan(groups):
    if groups == sum(GATHER):
        return GATHER, HIDDEN, RETURN, ORDER
    ones = (1,) * groups
    return ones, ones, ones, tuple((op, at) for at in range(groups) for op in "AFLUDHE")


def farthest_first(ny, nz):
    def hops(step, size):
        return min(step, size - step)

    order = sorted((-hops(dy, ny) - hops(dz, nz), dy, dz) for dy in range(ny) for dz in range(nz))
    return [(dy, dz) for _, dy, dz in order[:-1]]


def shifts_of(ny, nz):
    far = farthest_first(ny, nz)
    parts = [far[at::4] for at in range(4)]
    parts = sorted(parts, key=len)
    return [(0, 0)] + [shift for part in parts for shift in part]


def layer_kernel(
    dims, pieces, order,
    patches_hbm, ids_hbm, gates_hbm, up_hbm, down_hbm,
    out_ref,
    patches_v, ids_v, gates_v, up_v, down_v, up_t, down_t, down_all,
    onehot, send, rows_in, feats, hid, acc, sums, half_l, half_r, full_l, full_r, back, rows_out,
    in_sem, a2a_send, a2a_recv, back_send, back_recv, send_sem, recv_sem,
):
    ny, nz, nt, cap, dsh, hidden = dims
    gather_at, hidden_at, return_at = pieces
    experts = ny * nz
    nx = nt // 2
    count = ids_v.shape[1]
    slots = experts * cap
    unit = ny * cap
    width = send.shape[1]
    cut = (dsh // 16 + 1) // 2 * 16

    e = lax.axis_index("expert")
    t = lax.axis_index("tensor")
    y, z = e // nz, e % nz
    x, core = t // 2, t % 2
    right = (t + 2) % nt
    left = (t + nt - 2) % nt
    sib = x * 2 + 1 - core

    loads = [
        pltpu.make_async_copy(src, dst, in_sem.at[i])
        for i, (src, dst) in enumerate((
            (ids_hbm, ids_v), (patches_hbm, patches_v.at[pl.ds(0, dsh)]), (gates_hbm, gates_v),
            (up_hbm, up_v), (down_hbm, down_v),
        ))
    ]
    for load in loads[:2]:
        load.start()

    barrier = pltpu.get_barrier_semaphore()

    for dy, dz in farthest_first(ny, nz):
        to = ((y + dy) % ny) * nz + (z + dz) % nz
        pl.semaphore_signal(barrier, inc=1, device_id={"expert": to}, device_id_type=MESH)
    for partner in (right, left, sib):
        pl.semaphore_signal(barrier, inc=1, device_id={"tensor": partner}, device_id_type=MESH)

    for load in loads[2:]:
        load.start()

    def shard_of(step, parity):
        return ((x + step) % nx) * 2 + parity

    shifts = shifts_of(ny, nz)

    def away(k):
        dy, dz = shifts[k]
        return ((y + dy) % ny) * nz + (z + dz) % nz

    def block(k):
        return pl.ds(k * cap, cap)

    def lanes(piece):
        start, size = piece
        return pl.ds(start * unit, size * unit)

    if width > dsh:
        patches_v[dsh:width, :] = jnp.zeros((width - dsh, count), BF16)
    earlier = (
        lax.broadcasted_iota(jnp.int32, (count, count), 0) < lax.broadcasted_iota(jnp.int32, (count, count), 1)
    ).astype(F32).astype(BF16)
    expert_row = lax.broadcasted_iota(jnp.int32, (experts, count), 0)
    targets = []
    taken = jnp.zeros((experts, 1), F32)
    loads[0].wait()
    for k in range(TOP):
        ids = ids_v[k:k + 1, :]
        hot = (expert_row == ids).astype(F32)
        before = jnp.dot(hot.astype(BF16), earlier, preferred_element_type=F32) + taken
        rank = jnp.sum(hot * before, axis=0, keepdims=True)
        taken = taken + jnp.sum(hot, axis=1, keepdims=True)
        targets.append(jnp.where(rank < cap, ids.astype(F32) * cap + rank, -1.0))
    loads[1].wait()

    tile = min(256, slots)

    offset = lax.broadcasted_iota(jnp.int32, (cap, count), 0)
    for start in range(0, slots, tile):
        held = range(start // cap, (start + tile) // cap)
        slot = jnp.concatenate([away(k) * cap + offset for k in held], axis=0).astype(F32)
        both = jnp.zeros((tile, count), F32)
        for k in range(TOP):
            hit = (slot == targets[k]).astype(F32)
            onehot[k, start:start + tile, :] = hit.astype(BF16)
            both = both + hit
        send[start:start + tile, :] = lax.dot_general(
            both.astype(BF16), patches_v[...], (((1,), (1,)), ((), ())), preferred_element_type=F32
        ).astype(BF16)

    pl.semaphore_wait(barrier, experts - 1 + 3)

    for index, (start, size) in enumerate(gather_at):
        for k in range(max(1, start * ny), (start + size) * ny):
            pltpu.make_async_remote_copy(
                src_ref=send.at[block(k)], dst_ref=rows_in.at[block(k)],
                send_sem=a2a_send, recv_sem=a2a_recv.at[index],
                device_id={"expert": away(k)}, device_id_type=MESH,
            ).start()
    rows_in[0:cap, :] = send[0:cap, :]

    def push(kind, c, src, dst, partner):
        return pltpu.make_async_remote_copy(
            src_ref=src, dst_ref=dst, send_sem=send_sem.at[kind, c], recv_sem=recv_sem.at[kind, c],
            device_id={"tensor": partner}, device_id_type=MESH,
        )

    def shard(step, parity, first=0, size=None):
        size = dsh if size is None else size
        return pl.ds(pl.multiple_of(shard_of(step, parity) * dsh + first, 16), size)

    theirs = pl.ds(hidden, hidden)
    down_copies = [
        push(SIB_DOWN, step, down_t.at[shard(step, 1 - core)], down_all.at[pl.ds(step * dsh, dsh), theirs], sib)
        for step in range(nx)
    ]
    loads[4].wait()
    down_t[...] = down_v[...].T
    for step in range(nx):
        down_copies[step].start()
        down_all[step * dsh:(step + 1) * dsh, 0:hidden] = down_t[shard(step, core), :]
    loads[3].wait()
    up_t[...] = up_v[...].T
    loads[2].wait()

    def gather_copy(kind, c):
        step, first, size, partner = {
            OWN_RA: (0, 0, cut, right),
            OWN_RB: (0, cut, dsh - cut, right),
            OWN_LA: (0, 0, cut, left),
            OWN_LB: (0, cut, dsh - cut, left),
            FWD_R: (nx - 1, 0, cut, right),
            FWD_L: (1, cut, dsh - cut, left),
            SIB_OWN: (0, 0, dsh, sib),
            SIB_L: (nx - 1, 0, dsh, sib),
            SIB_R: (1, 0, dsh, sib),
            SIB_FA: (2, 0, cut, sib),
            SIB_FB: (2, cut, dsh - cut, sib),
        }[kind]
        ref = feats.at[shard(step, core, first, size), lanes(gather_at[c])]
        return push(kind, c, ref, ref, partner)

    def hid_copy(c):
        at = lanes(hidden_at[c])
        return push(SIB_HID, c, hid.at[pl.ds(0, hidden), at], hid.at[theirs, at], sib)

    def sum_copy(kind, c):
        at = lanes(return_at[c])
        if kind == HALF_R:
            return push(kind, c, sums.at[2, pl.ds(0, cut), at], half_l.at[:, at], right)
        if kind == HALF_L:
            return push(kind, c, sums.at[2, pl.ds(cut, dsh - cut), at], half_r.at[:, at], left)
        place, ref, partner = (1, full_l, right) if kind in (SUM_RA, SUM_RB) else (0, full_r, left)
        rows = pl.ds(0, cut) if kind in (SUM_RA, SUM_LA) else pl.ds(cut, dsh - cut)
        return push(kind, c, sums.at[place, rows, at], ref.at[rows, at], partner)

    def arrive(c):
        start, size = gather_at[c]
        own = cap if start == 0 else 0
        ref = rows_in.at[pl.ds(start * unit + own, size * unit - own)]
        pltpu.make_async_copy(ref, ref, a2a_recv.at[c]).wait()
        turned = rows_in[start * unit:(start + size) * unit, :].T
        feats[shard(0, core), lanes(gather_at[c])] = turned[0:dsh, :]
        for kind in (OWN_RA, OWN_LB, OWN_RB, OWN_LA, SIB_OWN):
            gather_copy(kind, c).start()

    def forward(c):
        gather_copy(OWN_RA, c).wait_recv()
        gather_copy(FWD_R, c).start()
        gather_copy(OWN_LB, c).wait_recv()
        gather_copy(FWD_L, c).start()

    def to_sibling(c):
        gather_copy(OWN_RB, c).wait_recv()
        gather_copy(SIB_L, c).start()
        gather_copy(OWN_LA, c).wait_recv()
        gather_copy(SIB_R, c).start()
        gather_copy(FWD_R, c).wait_recv()
        gather_copy(SIB_FA, c).start()
        gather_copy(FWD_L, c).wait_recv()
        gather_copy(SIB_FB, c).start()

    gathered = set()

    def overlaps(piece, other):
        return piece[0] < other[0] + other[1] and other[0] < piece[0] + piece[1]

    def up(c):
        for i, piece in enumerate(gather_at):
            if overlaps(piece, hidden_at[c]) and i not in gathered:
                gathered.add(i)
                for kind in (SIB_OWN, SIB_L, SIB_R, SIB_FA, SIB_FB):
                    gather_copy(kind, i).wait_recv()
        at = lanes(hidden_at[c])
        hid[0:hidden, at] = gelu(jnp.dot(up_t[...], feats[:, at], preferred_element_type=F32)).astype(BF16)
        hid_copy(c).start()

    exchanged = set()

    def down(c):
        if not exchanged:
            for copy in down_copies:
                copy.wait_recv()
        for i, piece in enumerate(hidden_at):
            if overlaps(piece, return_at[c]) and i not in exchanged:
                exchanged.add(i)
                hid_copy(i).wait_recv()
        at = lanes(return_at[c])

        def term(step):
            return jnp.dot(down_all[step * dsh:(step + 1) * dsh, :], hid[:, at], preferred_element_type=F32)

        sums[2, :, at] = term(2).astype(BF16)
        sum_copy(HALF_R, c).start()
        sum_copy(HALF_L, c).start()
        one = term(1)
        sums[1, cut:dsh, at] = one[cut:dsh].astype(BF16)
        sum_copy(SUM_RB, c).start()
        acc[1, 0:cut, at] = one[0:cut]
        last = term(nx - 1)
        sums[0, 0:cut, at] = last[0:cut].astype(BF16)
        sum_copy(SUM_LA, c).start()
        acc[1, cut:dsh, at] = last[cut:dsh]
        acc[0, :, at] = term(0)

    def add_half(c):
        at = lanes(return_at[c])
        sum_copy(HALF_R, c).wait_recv()
        sums[1, 0:cut, at] = (acc[1, 0:cut, at] + half_l[:, at].astype(F32)).astype(BF16)
        sum_copy(SUM_RA, c).start()
        sum_copy(HALF_L, c).wait_recv()
        sums[0, cut:dsh, at] = (acc[1, cut:dsh, at] + half_r[:, at].astype(F32)).astype(BF16)
        sum_copy(SUM_LB, c).start()

    def finish(c):
        start, size = return_at[c]
        at = lanes(return_at[c])
        for kind in (SUM_RA, SUM_RB, SUM_LA, SUM_LB):
            sum_copy(kind, c).wait_recv()
        done = acc[0, :, at] + full_l[:, at].astype(F32) + full_r[:, at].astype(F32)
        if width > dsh:
            done = jnp.concatenate([done, jnp.zeros((width - dsh, size * unit), F32)], axis=0)
        back[start * unit:(start + size) * unit, :] = done.astype(BF16).T

        for k in range(max(1, start * ny), (start + size) * ny):
            dy, dz = shifts[k]
            to = ((y + ny - dy) % ny) * nz + (z + nz - dz) % nz
            pltpu.make_async_remote_copy(
                src_ref=back.at[block(k)], dst_ref=rows_out.at[block(k)],
                send_sem=back_send, recv_sem=back_recv.at[c],
                device_id={"expert": to}, device_id_type=MESH,
            ).start()

    stages = dict(A=arrive, F=forward, L=to_sibling, U=up, D=down, H=add_half, E=finish)
    for op, c in order:
        stages[op](c)

    rows_out[0:cap, :] = back[0:cap, :]
    for copy in down_copies:
        copy.wait_send()
    for c in range(len(gather_at)):
        for kind in range(SIB_HID):
            gather_copy(kind, c).wait_send()
    for c in range(len(hidden_at)):
        hid_copy(c).wait_send()
    for c in range(len(return_at)):
        for kind in (HALF_R, HALF_L, SUM_RA, SUM_RB, SUM_LA, SUM_LB):
            sum_copy(kind, c).wait_send()
    rest = pl.ds(0, slots - cap)
    pltpu.make_async_copy(send.at[rest], send.at[rest], a2a_send).wait()
    pltpu.make_async_copy(back.at[rest], back.at[rest], back_send).wait()

    total = jnp.zeros((dsh, count), F32)
    for c, (start, size) in enumerate(return_at):
        own = cap if start == 0 else 0
        ref = rows_out.at[pl.ds(start * unit + own, size * unit - own)]
        pltpu.make_async_copy(ref, ref, back_recv.at[c]).wait()
        rows = slice(start * unit, (start + size) * unit)
        turned = rows_out[rows, :].T[0:dsh, :]
        for k in range(TOP):
            total = total + gates_v[k:k + 1, :] * jnp.dot(turned, onehot[k, rows, :], preferred_element_type=F32)
    out_ref[...] = total.astype(BF16)


def local(patches, expert_ids, gate_values, w_up, w_down):
    experts = lax.axis_size("expert")
    nt = lax.axis_size("tensor")
    count, dsh = patches.shape
    width = (dsh + 127) // 128 * 128
    model, hidden = w_up.shape[1:]
    cap = 21 * TOP * count // (20 * experts)
    slots = experts * cap
    ny = next(n for n in range(1, experts + 1) if n * n >= experts)
    nz = experts // ny
    nx = nt // 2
    cut = (dsh // 16 + 1) // 2 * 16
    gather, hiddens, returns, order = plan(nz)
    pieces = tuple(pieces_of(sizes) for sizes in (gather, hiddens, returns))
    most = max(nx, *(len(p) for p in pieces))
    hbm = pl.BlockSpec(memory_space=pl.ANY)
    dma = pltpu.SemaphoreType.DMA
    mixed = pl.pallas_call(
        functools.partial(layer_kernel, (ny, nz, nt, cap, dsh, hidden), pieces, order),
        out_shape=jax.ShapeDtypeStruct((dsh, count), BF16),
        in_specs=[hbm] * 5,
        out_specs=pl.BlockSpec(memory_space=pltpu.VMEM),
        scratch_shapes=[
            pltpu.VMEM((width, count), BF16),
            pltpu.VMEM((TOP, count), jnp.int32),
            pltpu.VMEM((TOP, count), F32),
            pltpu.VMEM((model, hidden), BF16),
            pltpu.VMEM((hidden, model), BF16),
            pltpu.VMEM((hidden, model), BF16),
            pltpu.VMEM((model, hidden), BF16),
            pltpu.VMEM((nx * dsh, 2 * hidden), BF16),
            pltpu.VMEM((TOP, slots, count), BF16),
            pltpu.VMEM((slots, width), BF16),
            pltpu.VMEM((slots, width), BF16),
            pltpu.VMEM((model, slots), BF16),
            pltpu.VMEM((2 * hidden, slots), BF16),
            pltpu.VMEM((2, dsh, slots), F32),
            pltpu.VMEM((3, dsh, slots), BF16),
            pltpu.VMEM((cut, slots), BF16),
            pltpu.VMEM((dsh - cut, slots), BF16),
            pltpu.VMEM((dsh, slots), BF16),
            pltpu.VMEM((dsh, slots), BF16),
            pltpu.VMEM((slots, width), BF16),
            pltpu.VMEM((slots, width), BF16),
            dma((5,)),
            dma,
            dma((len(gather),)),
            dma,
            dma((len(returns),)),
            dma((KINDS, most)),
            dma((KINDS, most)),
        ],
        compiler_params=pltpu.CompilerParams(
            collective_id=0, has_side_effects=True, vmem_limit_bytes=VMEM_LIMIT
        ),
        cost_estimate=pl.CostEstimate(
            flops=4 * slots * model * hidden, bytes_accessed=4 * model * hidden, transcendentals=0
        ),
    )(patches.T, expert_ids.T, gate_values.T, w_up[0], w_down[0])
    return mixed.T


def solution(mesh):
    in_specs = (
        P("expert", "tensor"),
        P("expert", None),
        P("expert", None),
        P("expert", None, "tensor"),
        P("expert", "tensor", None),
    )
    out_specs = P("expert", "tensor")
    return jax.shard_map(local, mesh=mesh, in_specs=in_specs, out_specs=out_specs, check_vma=False)
```

```python
import functools

import jax
import jax.numpy as jnp
from jax import lax
from jax.experimental import pallas as pl
from jax.experimental.pallas import tpu as pltpu
from jax.sharding import PartitionSpec as P

TOP = 2
VMEM_LIMIT = 60 * 1024 * 1024
MESH = pl.DeviceIdType.MESH
BF16 = jnp.bfloat16
F32 = jnp.float32

OWN_RA, OWN_RB, OWN_LA, OWN_LB, FWD_R, FWD_L, SIB_OWN, SIB_L, SIB_R, SIB_FA, SIB_FB = range(11)
SIB_HID, HALF_R, HALF_L, SUM_RA, SUM_RB, SUM_LA, SUM_LB, SIB_DOWN = range(11, 19)
KINDS = 19

GATHER = (2, 2, 2, 2)
HIDDEN = (2, 2, 2, 2)
RETURN = (2, 2, 2, 2)
ORDER = (
    ("A", 0), ("A", 1), ("F", 0), ("A", 2), ("F", 1), ("L", 0),
    ("A", 3), ("U", 0), ("F", 2), ("L", 1), ("U", 1), ("F", 3),
    ("D", 0), ("L", 2), ("D", 1), ("L", 3), ("U", 2), ("H", 0),
    ("D", 2), ("U", 3), ("H", 1), ("E", 0), ("D", 3), ("H", 2),
    ("E", 1), ("H", 3), ("E", 2), ("E", 3),
)


def gelu(x):
    return 0.5 * x * (1.0 + lax.erf(x * 0.7071067811865476))


def pieces_of(sizes):
    starts = [sum(sizes[:i]) for i in range(len(sizes))]
    return list(zip(starts, sizes))


def plan(groups):
    if groups == sum(GATHER):
        return GATHER, HIDDEN, RETURN, ORDER
    ones = (1,) * groups
    return ones, ones, ones, tuple((op, at) for at in range(groups) for op in "AFLUDHE")


def farthest_first(ny, nz):
    def hops(step, size):
        return min(step, size - step)

    order = sorted((-hops(dy, ny) - hops(dz, nz), dy, dz) for dy in range(ny) for dz in range(nz))
    return [(dy, dz) for _, dy, dz in order[:-1]]


def shifts_of(ny, nz):
    far = farthest_first(ny, nz)
    parts = [far[at::4] for at in range(4)]
    parts = sorted(parts, key=len)
    return [(0, 0)] + [shift for part in parts for shift in part]


def layer_kernel(
    dims, pieces, order,
    patches_hbm, ids_hbm, gates_hbm, up_hbm, down_hbm,
    out_ref,
    patches_v, ids_v, gates_v, up_v, down_v, up_t, down_t, down_all,
    onehot, send, rows_in, feats, hid, acc, sums, half_l, half_r, full_l, full_r, back, rows_out,
    in_sem, a2a_send, a2a_recv, back_send, back_recv, send_sem, recv_sem,
):
    ny, nz, nt, cap, dsh, hidden = dims
    gather_at, hidden_at, return_at = pieces
    experts = ny * nz
    nx = nt // 2
    count = ids_v.shape[1]
    slots = experts * cap
    unit = ny * cap
    width = send.shape[1]
    cut = (dsh // 16 + 1) // 2 * 16

    e = lax.axis_index("expert")
    t = lax.axis_index("tensor")
    y, z = e // nz, e % nz
    x, core = t // 2, t % 2
    right = (t + 2) % nt
    left = (t + nt - 2) % nt
    sib = x * 2 + 1 - core

    loads = [
        pltpu.make_async_copy(src, dst, in_sem.at[i])
        for i, (src, dst) in enumerate((
            (ids_hbm, ids_v), (patches_hbm, patches_v.at[pl.ds(0, dsh)]), (gates_hbm, gates_v),
            (up_hbm, up_v), (down_hbm, down_v),
        ))
    ]
    for load in loads[:2]:
        load.start()

    barrier = pltpu.get_barrier_semaphore()

    for dy, dz in farthest_first(ny, nz):
        to = ((y + dy) % ny) * nz + (z + dz) % nz
        pl.semaphore_signal(barrier, inc=1, device_id={"expert": to}, device_id_type=MESH)
    for partner in (right, left, sib):
        pl.semaphore_signal(barrier, inc=1, device_id={"tensor": partner}, device_id_type=MESH)

    for load in loads[2:]:
        load.start()

    def shard_of(step, parity):
        return ((x + step) % nx) * 2 + parity

    shifts = shifts_of(ny, nz)

    def away(k):
        dy, dz = shifts[k]
        return ((y + dy) % ny) * nz + (z + dz) % nz

    def block(k):
        return pl.ds(k * cap, cap)

    def lanes(piece):
        start, size = piece
        return pl.ds(start * unit, size * unit)

    if width > dsh:
        patches_v[dsh:width, :] = jnp.zeros((width - dsh, count), BF16)
    earlier = (
        lax.broadcasted_iota(jnp.int32, (count, count), 0) < lax.broadcasted_iota(jnp.int32, (count, count), 1)
    ).astype(F32).astype(BF16)
    expert_row = lax.broadcasted_iota(jnp.int32, (experts, count), 0)
    targets = []
    taken = jnp.zeros((experts, 1), F32)
    loads[0].wait()
    for k in range(TOP):
        ids = ids_v[k:k + 1, :]
        hot = (expert_row == ids).astype(F32)
        before = jnp.dot(hot.astype(BF16), earlier, preferred_element_type=F32) + taken
        rank = jnp.sum(hot * before, axis=0, keepdims=True)
        taken = taken + jnp.sum(hot, axis=1, keepdims=True)
        targets.append(jnp.where(rank < cap, ids.astype(F32) * cap + rank, -1.0))
    loads[1].wait()

    tile = min(256, slots)

    offset = lax.broadcasted_iota(jnp.int32, (cap, count), 0)
    for start in range(0, slots, tile):
        held = range(start // cap, (start + tile) // cap)
        slot = jnp.concatenate([away(k) * cap + offset for k in held], axis=0).astype(F32)
        both = jnp.zeros((tile, count), F32)
        for k in range(TOP):
            hit = (slot == targets[k]).astype(F32)
            onehot[k, start:start + tile, :] = hit.astype(BF16)
            both = both + hit
        send[start:start + tile, :] = lax.dot_general(
            both.astype(BF16), patches_v[...], (((1,), (1,)), ((), ())), preferred_element_type=F32
        ).astype(BF16)

    pl.semaphore_wait(barrier, experts - 1 + 3)

    for index, (start, size) in enumerate(gather_at):
        for k in range(max(1, start * ny), (start + size) * ny):
            pltpu.make_async_remote_copy(
                src_ref=send.at[block(k)], dst_ref=rows_in.at[block(k)],
                send_sem=a2a_send, recv_sem=a2a_recv.at[index],
                device_id={"expert": away(k)}, device_id_type=MESH,
            ).start()
    rows_in[0:cap, :] = send[0:cap, :]

    def push(kind, c, src, dst, partner):
        return pltpu.make_async_remote_copy(
            src_ref=src, dst_ref=dst, send_sem=send_sem.at[kind, c], recv_sem=recv_sem.at[kind, c],
            device_id={"tensor": partner}, device_id_type=MESH,
        )

    def shard(step, parity, first=0, size=None):
        size = dsh if size is None else size
        return pl.ds(pl.multiple_of(shard_of(step, parity) * dsh + first, 16), size)

    theirs = pl.ds(hidden, hidden)
    down_copies = [
        push(SIB_DOWN, step, down_t.at[shard(step, 1 - core)], down_all.at[pl.ds(step * dsh, dsh), theirs], sib)
        for step in range(nx)
    ]
    loads[4].wait()
    down_t[...] = down_v[...].T
    for step in range(nx):
        down_copies[step].start()
        down_all[step * dsh:(step + 1) * dsh, 0:hidden] = down_t[shard(step, core), :]
    loads[3].wait()
    up_t[...] = up_v[...].T
    loads[2].wait()

    def gather_copy(kind, c):
        step, first, size, partner = {
            OWN_RA: (0, 0, cut, right),
            OWN_RB: (0, cut, dsh - cut, right),
            OWN_LA: (0, 0, cut, left),
            OWN_LB: (0, cut, dsh - cut, left),
            FWD_R: (nx - 1, 0, cut, right),
            FWD_L: (1, cut, dsh - cut, left),
            SIB_OWN: (0, 0, dsh, sib),
            SIB_L: (nx - 1, 0, dsh, sib),
            SIB_R: (1, 0, dsh, sib),
            SIB_FA: (2, 0, cut, sib),
            SIB_FB: (2, cut, dsh - cut, sib),
        }[kind]
        ref = feats.at[shard(step, core, first, size), lanes(gather_at[c])]
        return push(kind, c, ref, ref, partner)

    def hid_copy(c):
        at = lanes(hidden_at[c])
        return push(SIB_HID, c, hid.at[pl.ds(0, hidden), at], hid.at[theirs, at], sib)

    def sum_copy(kind, c):
        at = lanes(return_at[c])
        if kind == HALF_R:
            return push(kind, c, sums.at[2, pl.ds(0, cut), at], half_l.at[:, at], right)
        if kind == HALF_L:
            return push(kind, c, sums.at[2, pl.ds(cut, dsh - cut), at], half_r.at[:, at], left)
        place, ref, partner = (1, full_l, right) if kind in (SUM_RA, SUM_RB) else (0, full_r, left)
        rows = pl.ds(0, cut) if kind in (SUM_RA, SUM_LA) else pl.ds(cut, dsh - cut)
        return push(kind, c, sums.at[place, rows, at], ref.at[rows, at], partner)

    def arrive(c):
        start, size = gather_at[c]
        own = cap if start == 0 else 0
        ref = rows_in.at[pl.ds(start * unit + own, size * unit - own)]
        pltpu.make_async_copy(ref, ref, a2a_recv.at[c]).wait()
        turned = rows_in[start * unit:(start + size) * unit, :].T
        feats[shard(0, core), lanes(gather_at[c])] = turned[0:dsh, :]
        for kind in (OWN_RA, OWN_LB, OWN_RB, OWN_LA, SIB_OWN):
            gather_copy(kind, c).start()

    def forward(c):
        gather_copy(OWN_RA, c).wait_recv()
        gather_copy(FWD_R, c).start()
        gather_copy(OWN_LB, c).wait_recv()
        gather_copy(FWD_L, c).start()

    def to_sibling(c):
        gather_copy(OWN_RB, c).wait_recv()
        gather_copy(SIB_L, c).start()
        gather_copy(OWN_LA, c).wait_recv()
        gather_copy(SIB_R, c).start()
        gather_copy(FWD_R, c).wait_recv()
        gather_copy(SIB_FA, c).start()
        gather_copy(FWD_L, c).wait_recv()
        gather_copy(SIB_FB, c).start()

    gathered = set()

    def overlaps(piece, other):
        return piece[0] < other[0] + other[1] and other[0] < piece[0] + piece[1]

    def up(c):
        for i, piece in enumerate(gather_at):
            if overlaps(piece, hidden_at[c]) and i not in gathered:
                gathered.add(i)
                for kind in (SIB_OWN, SIB_L, SIB_R, SIB_FA, SIB_FB):
                    gather_copy(kind, i).wait_recv()
        at = lanes(hidden_at[c])
        hid[0:hidden, at] = gelu(jnp.dot(up_t[...], feats[:, at], preferred_element_type=F32)).astype(BF16)
        hid_copy(c).start()

    exchanged = set()

    def down(c):
        if not exchanged:
            for copy in down_copies:
                copy.wait_recv()
        for i, piece in enumerate(hidden_at):
            if overlaps(piece, return_at[c]) and i not in exchanged:
                exchanged.add(i)
                hid_copy(i).wait_recv()
        at = lanes(return_at[c])

        def term(step):
            return jnp.dot(down_all[step * dsh:(step + 1) * dsh, :], hid[:, at], preferred_element_type=F32)

        sums[2, :, at] = term(2).astype(BF16)
        sum_copy(HALF_R, c).start()
        sum_copy(HALF_L, c).start()
        one = term(1)
        sums[1, cut:dsh, at] = one[cut:dsh].astype(BF16)
        sum_copy(SUM_RB, c).start()
        acc[1, 0:cut, at] = one[0:cut]
        last = term(nx - 1)
        sums[0, 0:cut, at] = last[0:cut].astype(BF16)
        sum_copy(SUM_LA, c).start()
        acc[1, cut:dsh, at] = last[cut:dsh]
        acc[0, :, at] = term(0)

    def add_half(c):
        at = lanes(return_at[c])
        sum_copy(HALF_R, c).wait_recv()
        sums[1, 0:cut, at] = (acc[1, 0:cut, at] + half_l[:, at].astype(F32)).astype(BF16)
        sum_copy(SUM_RA, c).start()
        sum_copy(HALF_L, c).wait_recv()
        sums[0, cut:dsh, at] = (acc[1, cut:dsh, at] + half_r[:, at].astype(F32)).astype(BF16)
        sum_copy(SUM_LB, c).start()

    def finish(c):
        start, size = return_at[c]
        at = lanes(return_at[c])
        for kind in (SUM_RA, SUM_RB, SUM_LA, SUM_LB):
            sum_copy(kind, c).wait_recv()
        done = acc[0, :, at] + full_l[:, at].astype(F32) + full_r[:, at].astype(F32)
        if width > dsh:
            done = jnp.concatenate([done, jnp.zeros((width - dsh, size * unit), F32)], axis=0)
        back[start * unit:(start + size) * unit, :] = done.astype(BF16).T

        for k in range(max(1, start * ny), (start + size) * ny):
            dy, dz = shifts[k]
            to = ((y + ny - dy) % ny) * nz + (z + nz - dz) % nz
            pltpu.make_async_remote_copy(
                src_ref=back.at[block(k)], dst_ref=rows_out.at[block(k)],
                send_sem=back_send, recv_sem=back_recv.at[c],
                device_id={"expert": to}, device_id_type=MESH,
            ).start()

    stages = dict(A=arrive, F=forward, L=to_sibling, U=up, D=down, H=add_half, E=finish)
    for op, c in order:
        stages[op](c)

    rows_out[0:cap, :] = back[0:cap, :]
    for copy in down_copies:
        copy.wait_send()
    for c in range(len(gather_at)):
        for kind in range(SIB_HID):
            gather_copy(kind, c).wait_send()
    for c in range(len(hidden_at)):
        hid_copy(c).wait_send()
    for c in range(len(return_at)):
        for kind in (HALF_R, HALF_L, SUM_RA, SUM_RB, SUM_LA, SUM_LB):
            sum_copy(kind, c).wait_send()
    rest = pl.ds(0, slots - cap)
    pltpu.make_async_copy(send.at[rest], send.at[rest], a2a_send).wait()
    pltpu.make_async_copy(back.at[rest], back.at[rest], back_send).wait()

    total = jnp.zeros((dsh, count), F32)
    for c, (start, size) in enumerate(return_at):
        own = cap if start == 0 else 0
        ref = rows_out.at[pl.ds(start * unit + own, size * unit - own)]
        pltpu.make_async_copy(ref, ref, back_recv.at[c]).wait()
        rows = slice(start * unit, (start + size) * unit)
        turned = rows_out[rows, :].T[0:dsh, :]
        for k in range(TOP):
            total = total + gates_v[k:k + 1, :] * jnp.dot(turned, onehot[k, rows, :], preferred_element_type=F32)
    out_ref[...] = total.astype(BF16)


def local(patches, expert_ids, gate_values, w_up, w_down):
    experts = lax.axis_size("expert")
    nt = lax.axis_size("tensor")
    count, dsh = patches.shape
    width = (dsh + 127) // 128 * 128
    model, hidden = w_up.shape[1:]
    cap = 21 * TOP * count // (20 * experts)
    slots = experts * cap
    ny = next(n for n in range(1, experts + 1) if n * n >= experts)
    nz = experts // ny
    nx = nt // 2
    cut = (dsh // 16 + 1) // 2 * 16
    gather, hiddens, returns, order = plan(nz)
    pieces = tuple(pieces_of(sizes) for sizes in (gather, hiddens, returns))
    most = max(nx, *(len(p) for p in pieces))
    hbm = pl.BlockSpec(memory_space=pl.ANY)
    dma = pltpu.SemaphoreType.DMA
    mixed = pl.pallas_call(
        functools.partial(layer_kernel, (ny, nz, nt, cap, dsh, hidden), pieces, order),
        out_shape=jax.ShapeDtypeStruct((dsh, count), BF16),
        in_specs=[hbm] * 5,
        out_specs=pl.BlockSpec(memory_space=pltpu.VMEM),
        scratch_shapes=[
            pltpu.VMEM((width, count), BF16),
            pltpu.VMEM((TOP, count), jnp.int32),
            pltpu.VMEM((TOP, count), F32),
            pltpu.VMEM((model, hidden), BF16),
            pltpu.VMEM((hidden, model), BF16),
            pltpu.VMEM((hidden, model), BF16),
            pltpu.VMEM((model, hidden), BF16),
            pltpu.VMEM((nx * dsh, 2 * hidden), BF16),
            pltpu.VMEM((TOP, slots, count), BF16),
            pltpu.VMEM((slots, width), BF16),
            pltpu.VMEM((slots, width), BF16),
            pltpu.VMEM((model, slots), BF16),
            pltpu.VMEM((2 * hidden, slots), BF16),
            pltpu.VMEM((2, dsh, slots), F32),
            pltpu.VMEM((3, dsh, slots), BF16),
            pltpu.VMEM((cut, slots), BF16),
            pltpu.VMEM((dsh - cut, slots), BF16),
            pltpu.VMEM((dsh, slots), BF16),
            pltpu.VMEM((dsh, slots), BF16),
            pltpu.VMEM((slots, width), BF16),
            pltpu.VMEM((slots, width), BF16),
            dma((5,)),
            dma,
            dma((len(gather),)),
            dma,
            dma((len(returns),)),
            dma((KINDS, most)),
            dma((KINDS, most)),
        ],
        compiler_params=pltpu.CompilerParams(
            collective_id=0, has_side_effects=True, vmem_limit_bytes=VMEM_LIMIT
        ),
        cost_estimate=pl.CostEstimate(
            flops=4 * slots * model * hidden, bytes_accessed=4 * model * hidden, transcendentals=0
        ),
    )(patches.T, expert_ids.T, gate_values.T, w_up[0], w_down[0])
    return mixed.T


def solution(mesh):
    in_specs = (
        P("expert", "tensor"),
        P("expert", None),
        P("expert", None),
        P("expert", None, "tensor"),
        P("expert", "tensor", None),
    )
    out_specs = P("expert", "tensor")
    return jax.shard_map(local, mesh=mesh, in_specs=in_specs, out_specs=out_specs, check_vma=False)
```
